32 devices in a mesh: case: 2 (over y), clus: 4 (over z), quad: 4 (over x, core).
Axes of the slice: x: 2, y: 2, z: 4, core: 2. Of those that a mesh axis runs over, the one named last changes fastest.
Arguments:
- targets: float32 [64, 3, 512], P(('case', 'clus')), parts along dimension 0, may hold values from 0 to 0.3
- source_xyz: float32 [64, 4, 3, 512], P(('case', 'clus'), 'quad'), parts along dimension 0, may hold values from 0 to 0.3
- source_wts: float32 [64, 4, 512], P(('case', 'clus'), 'quad'), parts along dimension 0, may hold values from 0.005 to 0.05
- density: bfloat16 [64, 64, 512], P(('case', 'clus')), parts along dimension 0, may hold values from -6 to 6
- pairs: int32 [560, 2], P(('case', 'clus')), parts along dimension 0, may hold values from -1 to 31, as said below
- panel_count: int32 [64], P(('case', 'clus')), parts along dimension 0, may hold values from 256 to 512, as said below
Outputs:
- potential: float32 [64, 64, 512], P(('case', 'clus'), None, 'quad'), parts along dimension 0
The draws below stay inside these ranges and needn't reach their ends.
There are 2 independent parts, one for each index of `case`. The reference program is written for one: setup_inputs(seed, part) draws one part's arguments, and reference() takes and returns one part's arrays. A program takes and returns all parts, laid end to end along the dimension named above; each array names one. Nothing has to cross between parts.
Inputs may be any that keep to these rules, and one draw needn't show every extreme that they name: `pairs`: rows come in blocks of 70, one block a device along clus in order; the rows of device d name target clusters d * 8 to (d + 1) * 8 - 1 in column 0 and a source cluster in column 1; unused rows are (-1, -1) and stand after the used ones. The list is symmetric: (a, b) is a row exactly when (b, a) is; no row stands twice and every cluster is paired with itself. At most 2 rows of one device name source clusters of one other device, and some device has exactly 2 such rows for every other device. A cluster's first panel_count panels are live; some cluster has all 512.
All inputs are finite; a program needn't handle non-finite values.
Results may differ from the reference program's by a relative error of at most 0.0029.
Values may be sent and summed in bfloat16 or wider, within the bound.
A program may use at most 64 MiB of HBM per device.

```python
import math
import jax
import jax.numpy as jnp
from jax import lax

P_SIZE = 512
Q = 4
R = 32
CL_DEV = 8
SLOTS = 2
NC = 32
PAIR_DEV = 70


def draw_pairs(key, part):
    key_hub, key_law, key_pick, key_self = jax.random.split(key, 4)
    devices = NC // CL_DEV
    combos = CL_DEV * CL_DEV
    hub_device = jax.random.randint(key_hub, (), 0, devices)
    law_draw = jax.random.randint(key_law, (devices, devices), 0, 20)
    counts = jnp.where(law_draw < 11, 0, jnp.where(law_draw < 16, 1, 2))
    device_ids = jnp.arange(devices)
    near_hub = (device_ids[:, None] == hub_device) | (device_ids[None, :] == hub_device)
    counts = jnp.where(near_hub, SLOTS, jnp.minimum(counts, SLOTS))
    upper_mask = device_ids[:, None] < device_ids[None, :]
    counts = jnp.where(upper_mask, counts, 0)
    scores = jax.random.randint(key_pick, (devices, devices, combos), 0, 1 << 20) * combos + jnp.arange(combos)
    rank_table = jnp.argsort(jnp.argsort(scores, axis=2), axis=2)
    chosen = (rank_table < counts[:, :, None]).reshape(devices, devices, CL_DEV, CL_DEV)
    cross_pairs = chosen | jnp.transpose(chosen, (1, 0, 3, 2))
    coin_flips = jax.random.randint(key_self, (devices, CL_DEV, CL_DEV), 0, 10) == 0
    inner_ids = jnp.arange(CL_DEV)
    coin_flips = coin_flips & (inner_ids[:, None] < inner_ids[None, :])[None]
    own_pairs = coin_flips | jnp.transpose(coin_flips, (0, 2, 1)) | (inner_ids[:, None] == inner_ids[None, :])[None]
    same_device = (device_ids[:, None] == device_ids[None, :])[:, :, None, None]
    adjacency = cross_pairs | own_pairs[:, None] & same_device
    flat_adj = adjacency.reshape(devices, devices * combos)
    flat_index = jnp.arange(devices * combos)
    sort_keys = jnp.where(flat_adj, flat_index[None, :], devices * combos)
    sort_order = jnp.argsort(sort_keys, axis=1, stable=True)[:, :PAIR_DEV]
    taken_keys = jnp.take_along_axis(sort_keys, sort_order, axis=1)
    valid_rows = taken_keys < devices * combos
    peer_ids = taken_keys // combos
    local_pair = taken_keys % combos
    target = device_ids[:, None] * CL_DEV + local_pair // CL_DEV
    source = peer_ids * CL_DEV + local_pair % CL_DEV
    target = jnp.where(valid_rows, target, -1)
    source = jnp.where(valid_rows, source, -1)
    return jnp.stack([target, source], axis=-1).reshape(devices * PAIR_DEV, 2).astype(jnp.int32)


def draw_panel_count(key, part):
    key_count, key_full = jax.random.split(key)
    counts = jax.random.randint(key_count, (NC,), P_SIZE // 2, P_SIZE + 1)
    full_at = jax.random.randint(key_full, (), 0, NC)
    return counts.at[full_at].set(P_SIZE).astype(jnp.int32)


def levels(own_key, shape, cuts, low, high):
    level = 1.0
    for dim, parts in cuts:
        steps = jax.random.uniform(jax.random.fold_in(jax.random.fold_in(own_key, 6), dim), (parts,), jnp.float32, low / len(cuts), high / len(cuts))
        level = level * jnp.repeat(jnp.exp(steps), shape[dim] // parts).reshape((-1,) + (1,) * (len(shape) - 1 - dim))
    return level


def normal_values(key, dims, deviation, bound, cuts=(), kind=jnp.bfloat16):
    drawn = deviation * jax.random.normal(key, dims, jnp.float32)
    if cuts:
        drawn = drawn * levels(key, dims, cuts, -0.22, 0.18)
    return jnp.clip(drawn, -bound, bound).astype(kind)


def setup_inputs(seed: int = 0, part: int = 0) -> dict:
    streams_of = jax.random.split(jax.random.key(seed), 7)
    part_splits = jax.random.split(jax.random.fold_in(streams_of[6], part), 7)
    targets = jnp.clip(0.3 * jax.random.uniform(part_splits[0], (NC, 3, P_SIZE), jnp.float32) ** levels(part_splits[0], (NC, 3, P_SIZE), ((0, 4),), -0.2, 0.2), 0.0, 0.3)
    source_xyz = jnp.clip(0.3 * jax.random.uniform(part_splits[1], (NC, Q, 3, P_SIZE), jnp.float32) ** levels(part_splits[1], (NC, Q, 3, P_SIZE), ((0, 4), (1, 4)), -0.2, 0.2), 0.0, 0.3)
    source_wts = jnp.clip(jnp.exp(math.log(0.05) - 2.3025851 * jax.random.uniform(part_splits[2], (NC, Q, P_SIZE), jnp.float32) ** levels(part_splits[2], (NC, Q, P_SIZE), ((0, 4), (1, 4)), -0.2, 0.2)), 0.005, 0.05)
    density = normal_values(part_splits[3], (NC, 2 * R, P_SIZE), 1.0, 6.0, ((0, 4),))
    pairs = draw_pairs(jax.random.fold_in(jax.random.fold_in(streams_of[6], part), 71), part)
    panel_count = draw_panel_count(jax.random.fold_in(jax.random.fold_in(streams_of[6], part), 71), part)
    return dict(targets=targets, source_xyz=source_xyz, source_wts=source_wts, density=density, pairs=pairs, panel_count=panel_count)


MACH = 0.3
BETA_SQ = 1.0 - MACH * MACH
WAVE = 2.0 * math.pi * 8000.0 / 340.0
SOFT_SQ = 0.003 * 0.003
FOUR_PI = 4.0 * math.pi

def point_tile(target_xyz, point_xyz, point_wts):
    delta_x = target_xyz[0][:, None] - point_xyz[0][None, :]
    delta_y = target_xyz[1][:, None] - point_xyz[1][None, :]
    delta_z = target_xyz[2][:, None] - point_xyz[2][None, :]
    distance = jnp.sqrt(delta_x * delta_x + BETA_SQ * (delta_y * delta_y + delta_z * delta_z) + SOFT_SQ)
    phase_arg = WAVE * (distance - MACH * delta_x) / BETA_SQ
    amplitude = point_wts[None, :] / (FOUR_PI * distance)
    real_tile = (amplitude * jnp.cos(phase_arg)).astype(jnp.bfloat16)
    imag_tile = (amplitude * jnp.sin(phase_arg)).astype(jnp.bfloat16)
    return (real_tile, imag_tile)

def pair_term(target_xyz, source_pts, source_live_wts, sigma, target_live):
    half_rows = sigma.shape[0] // 2
    summed = jnp.zeros(sigma.shape, jnp.float32)
    for point_idx in range(source_pts.shape[0]):
        real_tile, imag_tile = point_tile(target_xyz, source_pts[point_idx], source_live_wts[point_idx])
        real_part = jnp.dot(sigma, real_tile.T, preferred_element_type=jnp.float32)
        imag_part = jnp.dot(sigma, imag_tile.T, preferred_element_type=jnp.float32)
        summed = summed + jnp.concatenate([real_part[:half_rows] - imag_part[half_rows:], real_part[half_rows:] + imag_part[:half_rows]], axis=0)
    return summed * target_live[None, :]

def reference(targets, source_xyz, source_wts, density, pairs, panel_count):
    clusters = targets.shape[0]
    panels = targets.shape[2]
    panel_index = jnp.arange(panels, dtype=jnp.int32)
    live_mask = (panel_index[None, :] < panel_count[:, None]).astype(jnp.float32)
    live_wts = source_wts * live_mask[:, None, :]

    def add_pair(summed, pair_row):
        target = jnp.maximum(pair_row[0], 0)
        source = jnp.maximum(pair_row[1], 0)

        def compute(current):
            term = pair_term(targets[target], source_xyz[source], live_wts[source], density[source], live_mask[target])
            return current.at[target].add(term)

        def keep_same(current):
            return current
        return (lax.cond(pair_row[0] >= 0, compute, keep_same, summed), None)
    initial = jnp.zeros((clusters, density.shape[1], panels), jnp.float32)
    summed, unused = lax.scan(add_pair, initial, pairs)
    return summed
```

```python
import functools
import math

import jax
import jax.numpy as jnp
import numpy as np
from jax import lax
from jax.experimental import pallas as pl
from jax.experimental.pallas import tpu as pltpu
from jax.sharding import PartitionSpec as P

SLOTS = 2
MACH = 0.3
BETA_SQ = 1.0 - MACH * MACH
TURNS = 8000.0 / 340.0 / BETA_SQ
SOFT = (0.003 * TURNS) ** 2
AMP = TURNS / (4.0 * math.pi)
MAGIC = 12582912.0
LANES = 128
CHUNK = 16


def fit_half_turn(count):
    z = 0.125 - 0.125 * np.cos(np.pi * (np.arange(200) + 0.5) / 200)
    f = np.sqrt(z)
    cheb = np.polynomial.chebyshev.Chebyshev
    poly = np.polynomial.Polynomial
    out = []
    for y in (np.sqrt(2) * np.sin(np.pi * f) / f, np.sqrt(2) * np.cos(np.pi * f)):
        fitted = cheb.fit(z, y, count - 1, domain=[0, 0.25])
        out.append([float(v) for v in fitted.convert(kind=poly).coef])
    return out


SIN_C, COS_C = fit_half_turn(4)


def horner(coefs, z):
    value = coefs[-1]
    for c in coefs[-2::-1]:
        value = value * z + c
    return value


def plan_kernel(
    clusters, peers, me_ref, pairs_ref, geom_ref, dens_ref,
    sgeom_ref, sdens_ref, ltgt, lsrc, rtgt, rsrc, counts, cnt, key, tgt,
):
    rows = pairs_ref.shape[0] // 2
    me = me_ref[0]
    first = me * clusters
    total = peers * clusters

    def clear(p, carry):
        cnt[p] = 0
        return carry

    lax.fori_loop(0, peers, clear, 0)

    def one_row(r, n_local):
        a = pairs_ref[2 * r]
        b = pairs_ref[2 * r + 1]
        used = a >= 0
        owner = lax.div(jnp.maximum(b, 0), jnp.int32(clusters))
        local = used & (owner == me)

        @pl.when(local)
        def _():
            ltgt[n_local] = a - first
            lsrc[n_local] = b - first

        @pl.when(used & (owner != me))
        def _():
            mine = jnp.minimum(a, b) * total + jnp.maximum(a, b)
            have = cnt[owner]
            base = owner * SLOTS
            front = (have > 0) & (mine < key[base])

            @pl.when(front)
            def _():
                key[base + 1] = key[base]
                tgt[base + 1] = tgt[base]

            at = jnp.where(front | (have == 0), base, base + 1)
            key[at] = mine
            tgt[at] = a - first
            cnt[owner] = have + 1

        return n_local + local.astype(jnp.int32)

    counts[0] = lax.fori_loop(0, rows, one_row, jnp.int32(0))

    def one_slot(i, n_remote):
        p = lax.div(i, jnp.int32(SLOTS))
        filled = (i - p * SLOTS) < cnt[p]

        @pl.when(filled)
        def _():
            c = tgt[i]
            sgeom_ref[i] = geom_ref[c]
            sdens_ref[i] = dens_ref[c]
            rtgt[n_remote] = c
            rsrc[n_remote] = i

        return n_remote + filled.astype(jnp.int32)

    counts[1] = lax.fori_loop(0, peers * SLOTS, one_slot, jnp.int32(0))


def pair_kernel(which, counts, tgt, src, nblk, *rest):
    if which == 0:
        tpts_ref, geom_ref, dens_ref, acc_ref, tb, tile = rest
    else:
        info, tpts_ref, geom_ref, dens_ref, prev_ref, out_ref, acc_ref, tb, tile = rest
    clusters, width = tpts_ref.shape[0], tpts_ref.shape[1]
    points = geom_ref.shape[0]

    def fill(c, carry):
        pts = tpts_ref[c]
        for k in range(3):
            tb[c, k] = jnp.broadcast_to(pts[:, k : k + 1], (width, LANES))
        if which == 0:
            acc_ref[c] = jnp.zeros(acc_ref.shape[1:], jnp.float32)
        else:
            acc_ref[c] = prev_ref[c]
        return carry

    lax.fori_loop(0, clusters, fill, 0)

    def one_pair(i, carry):
        t = tgt[i]
        s = src[i]

        def one_block(sb, inner):
            cols = pl.ds(pl.multiple_of(sb * LANES, LANES), LANES)
            for ch in range(width // CHUNK):
                rows = pl.ds(ch * CHUNK, CHUNK)
                tx, ty, tz = tb[t, 0, rows, :], tb[t, 1, rows, :], tb[t, 2, rows, :]
                re = im = None
                for q in range(points):
                    sx = geom_ref[q, s, pl.ds(0, 1), cols]
                    sy = geom_ref[q, s, pl.ds(1, 1), cols]
                    sz = geom_ref[q, s, pl.ds(2, 1), cols]
                    w = geom_ref[q, s, pl.ds(3, 1), cols]
                    dx, dy, dz = tx - sx, ty - sy, tz - sz
                    sq = dx * dx + (dy * dy + (dz * dz + SOFT))
                    inv = lax.rsqrt(sq)
                    turns = sq * inv - MACH * dx
                    f = turns - ((turns + MAGIC) - MAGIC)
                    z = f * f
                    sn = f * horner(SIN_C, z)
                    cs = horner(COS_C, z)
                    amp = w * inv
                    asn = amp * sn
                    kr = amp - asn * sn
                    ki = asn * cs
                    re = kr if re is None else re + kr
                    im = ki if im is None else im + ki
                tile[pl.ds(ch * CHUNK, CHUNK), :] = re.astype(jnp.bfloat16)
                tile[pl.ds(width + ch * CHUNK, CHUNK), :] = im.astype(jnp.bfloat16)
            acc_ref[t] += lax.dot_general(
                tile[...], dens_ref[s, :, cols], (((1,), (1,)), ((), ())),
                preferred_element_type=jnp.float32,
            )
            return inner

        lax.fori_loop(0, nblk[s], one_block, 0)
        return carry

    lax.fori_loop(0, counts[which], one_pair, 0)

    if which == 1:
        half = out_ref.shape[1] // 2
        lane = lax.broadcasted_iota(jnp.int32, (half, width), 1) + info[0] * width

        def finish(c, carry):
            live = lane < info[c + 1]
            p = acc_ref[c, pl.ds(0, width), :].T
            q = acc_ref[c, pl.ds(width, width), :].T
            out_ref[c, pl.ds(0, half), :] = jnp.where(live, p[:half] - q[half:], 0.0)
            out_ref[c, pl.ds(half, half), :] = jnp.where(live, p[half:] + q[:half], 0.0)
            return carry

        lax.fori_loop(0, clusters, finish, 0)


VM = pl.BlockSpec(memory_space=pltpu.VMEM)
SM = pl.BlockSpec(memory_space=pltpu.SMEM)
PARAMS = pltpu.CompilerParams(vmem_limit_bytes=40 << 20)


def run_pairs(which, lists, arrays, info, prev, rows, est):
    tpts, geom, dens = arrays
    clusters, width = tpts.shape[0], tpts.shape[1]
    acc_shape = (clusters, 2 * width, rows)
    scratch = [
        pltpu.VMEM((clusters, 3, width, LANES), jnp.float32),
        pltpu.VMEM((2 * width, LANES), jnp.bfloat16),
    ]
    work = pl.CostEstimate(flops=est, bytes_accessed=4 << 20, transcendentals=0)
    if which == 0:
        return pl.pallas_call(
            functools.partial(pair_kernel, 0),
            out_shape=jax.ShapeDtypeStruct(acc_shape, jnp.float32),
            in_specs=[SM] * 4 + [VM] * 3,
            out_specs=VM,
            scratch_shapes=scratch,
            compiler_params=PARAMS,
            cost_estimate=work,
        )(*lists, tpts, geom, dens)
    return pl.pallas_call(
        functools.partial(pair_kernel, 1),
        out_shape=jax.ShapeDtypeStruct((clusters, rows, width), jnp.float32),
        in_specs=[SM] * 5 + [VM] * 4,
        out_specs=VM,
        scratch_shapes=[pltpu.VMEM(acc_shape, jnp.float32)] + scratch,
        compiler_params=PARAMS,
        cost_estimate=work,
    )(*lists, info, tpts, geom, dens, prev)


def shards(targets, source_xyz, source_wts, density, pairs, panel_count):
    clusters, _, panels = targets.shape
    peers = lax.axis_size("clus")
    quads = lax.axis_size("quad")
    width = panels // quads
    rows = density.shape[1]
    quad = lax.axis_index("quad")
    beta = math.sqrt(BETA_SQ)
    scale = jnp.array([TURNS, TURNS * beta, TURNS * beta], jnp.float32)
    live = jnp.arange(panels, dtype=jnp.int32)[None, :] < panel_count[:, None]
    packed = jnp.concatenate(
        [
            source_xyz[:, 0] * scale[None, :, None],
            jnp.where(live, source_wts[:, 0] * AMP, 0.0)[:, None, :],
        ],
        axis=1,
    )
    mine = lax.dynamic_slice_in_dim(targets, quad * width, width, 2)
    tpts = jnp.transpose(mine * scale[None, :, None], (0, 2, 1))
    me = lax.axis_index("clus").astype(jnp.int32).reshape(1)
    slots = peers * SLOTS
    row_count = pairs.shape[0]
    i32 = jnp.int32
    sgeom, sdens, ltgt, lsrc, rtgt, rsrc, counts = pl.pallas_call(
        functools.partial(plan_kernel, clusters, peers),
        out_shape=(
            jax.ShapeDtypeStruct((slots,) + packed.shape[1:], jnp.float32),
            jax.ShapeDtypeStruct((slots,) + density.shape[1:], density.dtype),
            jax.ShapeDtypeStruct((row_count,), i32),
            jax.ShapeDtypeStruct((row_count,), i32),
            jax.ShapeDtypeStruct((slots,), i32),
            jax.ShapeDtypeStruct((slots,), i32),
            jax.ShapeDtypeStruct((2,), i32),
        ),
        in_specs=[SM, SM, VM, VM],
        out_specs=(VM, VM, SM, SM, SM, SM, SM),
        scratch_shapes=[
            pltpu.SMEM((peers,), i32),
            pltpu.SMEM((slots,), i32),
            pltpu.SMEM((slots,), i32),
        ],
        compiler_params=PARAMS,
    )(me, pairs.reshape(-1), packed, density)
    own_geom = lax.all_gather(packed, "quad", axis=0)
    rgeom = lax.all_to_all(sgeom, "clus", split_axis=0, concat_axis=0, tiled=True)
    rdens = lax.all_to_all(sdens, "clus", split_axis=0, concat_axis=0, tiled=True)
    far_geom = lax.all_gather(rgeom, "quad", axis=0)
    own_blocks = (panel_count + (LANES - 1)) // LANES
    block_no = jnp.arange(panels, dtype=i32) // LANES + 1
    far_blocks = jnp.max(jnp.where(rgeom[:, 3, :] != 0, block_no[None, :], 0), axis=1)
    info = jnp.concatenate([quad.astype(i32).reshape(1), panel_count])
    near = run_pairs(
        0, (counts, ltgt, lsrc, own_blocks), (tpts, own_geom, density), None, None, rows, 16 << 30
    )
    return run_pairs(
        1, (counts, rtgt, rsrc, far_blocks), (tpts, far_geom, rdens), info, near, rows, 6 << 30
    )


def solution(mesh):
    return jax.shard_map(
        shards,
        mesh=mesh,
        in_specs=(
            P(("case", "clus"), None, None),
            P(("case", "clus"), "quad", None, None),
            P(("case", "clus"), "quad", None),
            P(("case", "clus"), None, None),
            P(("case", "clus"), None),
            P(("case", "clus")),
        ),
        out_specs=P(("case", "clus"), None, "quad"),
        check_vma=False,
    )
```

```python
import functools
import math

import jax
import jax.numpy as jnp
import numpy as np
from jax import lax
from jax.experimental import pallas as pl
from jax.experimental.pallas import tpu as pltpu
from jax.sharding import PartitionSpec as P

SLOTS = 2
MACH = 0.3
BETA_SQ = 1.0 - MACH * MACH
TURNS = 8000.0 / 340.0 / BETA_SQ
SOFT = (0.003 * TURNS) ** 2
AMP = TURNS / (4.0 * math.pi)
MAGIC = 12582912.0
LANES = 128
CHUNK = 16


def fit_half_turn(count):
    z = 0.125 - 0.125 * np.cos(np.pi * (np.arange(200) + 0.5) / 200)
    f = np.sqrt(z)
    cheb = np.polynomial.chebyshev.Chebyshev
    poly = np.polynomial.Polynomial
    out = []
    for y in (np.sqrt(2) * np.sin(np.pi * f) / f, np.sqrt(2) * np.cos(np.pi * f)):
        fitted = cheb.fit(z, y, count - 1, domain=[0, 0.25])
        out.append([float(v) for v in fitted.convert(kind=poly).coef])
    return out


SIN_C, COS_C = fit_half_turn(4)


def horner(coefs, z):
    value = coefs[-1]
    for c in coefs[-2::-1]:
        value = value * z + c
    return value


def plan_kernel(
    clusters, peers, me_ref, pairs_ref, geom_ref, dens_ref,
    send_ref, ltgt, lsrc, rtgt, rsrc, counts, cnt, key, tgt,
):
    rows = pairs_ref.shape[0] // 2
    drows = dens_ref.shape[1]
    me = me_ref[0]
    first = me * clusters
    total = peers * clusters

    def clear(p, carry):
        cnt[p] = 0
        return carry

    lax.fori_loop(0, peers, clear, 0)

    def more(state):
        return (state[0] < rows) & (pairs_ref[jnp.minimum(state[0], rows - 1)] >= 0)

    def one_row(state):
        r, n_local = state
        a = pairs_ref[r]
        b = pairs_ref[rows + r]
        owner = lax.div(b, jnp.int32(clusters))
        local = owner == me

        @pl.when(local)
        def _():
            ltgt[n_local] = a - first
            lsrc[n_local] = b - first

        @pl.when(owner != me)
        def _():
            mine = jnp.minimum(a, b) * total + jnp.maximum(a, b)
            have = cnt[owner]
            base = owner * SLOTS
            front = (have > 0) & (mine < key[base])

            @pl.when(front)
            def _():
                key[base + 1] = key[base]
                tgt[base + 1] = tgt[base]

            at = jnp.where(front | (have == 0), base, base + 1)
            key[at] = mine
            tgt[at] = a - first
            cnt[owner] = have + 1

        return r + 1, n_local + local.astype(jnp.int32)

    counts[0] = lax.while_loop(more, one_row, (jnp.int32(0), jnp.int32(0)))[1]

    def one_slot(i, n_remote):
        p = lax.div(i, jnp.int32(SLOTS))
        filled = (i - p * SLOTS) < cnt[p]

        @pl.when(filled)
        def _():
            c = tgt[i]
            send_ref[i, pl.ds(0, drows), :] = dens_ref[c]
            rest = jnp.concatenate([geom_ref[q, c] for q in range(geom_ref.shape[0])], axis=0)
            for part in range(3):
                piece = rest.astype(jnp.bfloat16)
                send_ref[i, pl.ds(drows + part * rest.shape[0], rest.shape[0]), :] = piece
                rest = rest - piece.astype(jnp.float32)
            rtgt[n_remote] = c
            rsrc[n_remote] = i

        return n_remote + filled.astype(jnp.int32)

    counts[1] = lax.fori_loop(0, peers * SLOTS, one_slot, jnp.int32(0))


def pair_kernel(which, points, counts, tgt, src, *rest):
    if which == 0:
        nblk, tpts_ref, geom_ref, dens_ref, acc_ref, tb, tile_a, tile_b = rest
    else:
        (info, tpts_ref, dens_ref, prev_ref, out_ref, acc_ref, tb, tile_a, tile_b, geom_ref,
         nblk) = rest
    clusters, width = tpts_ref.shape[0], tpts_ref.shape[1]
    quarter = width // 2
    drows = acc_ref.shape[2]
    tiles = (tile_a, tile_b)

    def source(q, s, comp, cols):
        if which == 0:
            return geom_ref[q, s, pl.ds(comp, 1), cols]
        return geom_ref[s, pl.ds(4 * q + comp, 1), cols]

    def unpack(i, carry):
        s = src[i]
        n = 4 * points
        p0, p1, p2 = [dens_ref[s, pl.ds(drows + k * n, n), :].astype(jnp.float32) for k in range(3)]
        whole = p0 + (p1 + p2)
        geom_ref[s] = whole
        block_no = lax.broadcasted_iota(jnp.int32, whole.shape, 1) // LANES + 1
        weight_row = lax.rem(lax.broadcasted_iota(jnp.int32, whole.shape, 0), 4) == 3
        reach = jnp.where(weight_row & (whole != 0), block_no.astype(jnp.float32), 0.0)
        nblk[s] = jnp.max(reach).astype(jnp.int32)
        return carry

    if which == 1:
        lax.fori_loop(0, counts[1], unpack, 0)

    def fill(c, carry):
        pts = tpts_ref[c]
        for k in range(3):
            tb[c, k] = jnp.broadcast_to(pts[:, k : k + 1], (width, LANES))
        if which == 0:
            acc_ref[c] = jnp.zeros(acc_ref.shape[1:], jnp.float32)
        else:
            acc_ref[c] = prev_ref[c]
        return carry

    lax.fori_loop(0, clusters, fill, 0)

    def one_pair(i, carry):
        t = tgt[i]
        s = src[i]

        def one_block(sb, inner):
            cols = pl.ds(pl.multiple_of(sb * LANES, LANES), LANES)
            for ch in range(width // CHUNK):
                rows = pl.ds(ch * CHUNK, CHUNK)
                tx, ty, tz = tb[t, 0, rows, :], tb[t, 1, rows, :], tb[t, 2, rows, :]
                re = im = None
                for q in range(points):
                    sx = source(q, s, 0, cols)
                    sy = source(q, s, 1, cols)
                    sz = source(q, s, 2, cols)
                    w = source(q, s, 3, cols)
                    dx, dy, dz = tx - sx, ty - sy, tz - sz
                    sq = dx * dx + (dy * dy + (dz * dz + SOFT))
                    inv = lax.rsqrt(sq)
                    turns = sq * inv - MACH * dx
                    f = turns - ((turns + MAGIC) - MAGIC)
                    z = f * f
                    sn = f * horner(SIN_C, z)
                    cs = horner(COS_C, z)
                    amp = w * inv
                    asn = amp * sn
                    kr = amp - asn * sn
                    ki = asn * cs
                    re = kr if re is None else re + kr
                    im = ki if im is None else im + ki
                tile = tiles[ch * CHUNK // quarter]
                at = ch * CHUNK % quarter
                tile[pl.ds(at, CHUNK), :] = re.astype(jnp.bfloat16)
                tile[pl.ds(quarter + at, CHUNK), :] = im.astype(jnp.bfloat16)
                if at + CHUNK == quarter:
                    part = pl.ds(ch * CHUNK // quarter * width, width)
                    acc_ref[t, part, :] += lax.dot_general(
                        tile[...], dens_ref[s, pl.ds(0, drows), cols], (((1,), (1,)), ((), ())),
                        preferred_element_type=jnp.float32,
                    )
            return inner

        lax.fori_loop(0, nblk[s], one_block, 0)
        return carry

    lax.fori_loop(0, counts[which], one_pair, 0)

    if which == 1:
        half = out_ref.shape[1] // 2
        lane = lax.broadcasted_iota(jnp.int32, (half, width), 1) + info[0] * width

        def finish(c, carry):
            live = lane < info[c + 1]
            p, q = [
                jnp.concatenate(
                    [acc_ref[c, pl.ds(g * width + o, quarter), :] for g in range(2)], axis=0
                ).T
                for o in (0, quarter)
            ]
            out_ref[c, pl.ds(0, half), :] = jnp.where(live, p[:half] - q[half:], 0.0)
            out_ref[c, pl.ds(half, half), :] = jnp.where(live, p[half:] + q[:half], 0.0)
            return carry

        lax.fori_loop(0, clusters, finish, 0)


VM = pl.BlockSpec(memory_space=pltpu.VMEM)
SM = pl.BlockSpec(memory_space=pltpu.SMEM)
PARAMS = pltpu.CompilerParams(vmem_limit_bytes=40 << 20)


def run_pairs(which, points, lists, arrays, est):
    tpts, dens = arrays[0], arrays[-1] if which == 0 else arrays[1]
    clusters, width = tpts.shape[0], tpts.shape[1]
    panels = dens.shape[2]
    rows = dens.shape[1] - (12 * points if which == 1 else 0)
    acc_shape = (clusters, 2 * width, rows)
    scratch = [
        pltpu.VMEM((clusters, 3, width, LANES), jnp.float32),
        pltpu.VMEM((width, LANES), jnp.bfloat16),
        pltpu.VMEM((width, LANES), jnp.bfloat16),
    ]
    out_shape = acc_shape
    if which == 1:
        out_shape = (clusters, rows, width)
        scratch = [pltpu.VMEM(acc_shape, jnp.float32)] + scratch + [
            pltpu.VMEM((dens.shape[0], 4 * points, panels), jnp.float32),
            pltpu.SMEM((dens.shape[0],), jnp.int32),
        ]
    return pl.pallas_call(
        functools.partial(pair_kernel, which, points),
        out_shape=jax.ShapeDtypeStruct(out_shape, jnp.float32),
        in_specs=[SM] * len(lists) + [VM] * len(arrays),
        out_specs=VM,
        scratch_shapes=scratch,
        compiler_params=PARAMS,
        cost_estimate=pl.CostEstimate(flops=est, bytes_accessed=4 << 20, transcendentals=0),
    )(*lists, *arrays)


def shards(targets, source_xyz, source_wts, density, pairs, panel_count):
    clusters, _, panels = targets.shape
    peers = lax.axis_size("clus")
    quads = lax.axis_size("quad")
    width = panels // quads
    rows = density.shape[1]
    quad = lax.axis_index("quad")
    i32 = jnp.int32
    comp = lax.broadcasted_iota(i32, (1, 3, 1), 1)
    scale = jnp.where(comp == 0, jnp.float32(TURNS), jnp.float32(TURNS * math.sqrt(BETA_SQ)))
    live = jnp.arange(panels, dtype=i32)[None, :] < panel_count[:, None]
    packed = jnp.concatenate(
        [
            source_xyz[:, 0] * scale,
            jnp.where(live, source_wts[:, 0] * AMP, 0.0)[:, None, :],
        ],
        axis=1,
    )
    own_geom = lax.all_gather(packed, "quad", axis=0)
    mine = lax.dynamic_slice_in_dim(targets, quad * width, width, 2)
    tpts = jnp.transpose(mine * scale, (0, 2, 1))
    me = lax.axis_index("clus").astype(i32).reshape(1)
    slots = peers * SLOTS
    row_count = pairs.shape[0]
    send, ltgt, lsrc, rtgt, rsrc, counts = pl.pallas_call(
        functools.partial(plan_kernel, clusters, peers),
        out_shape=(
            jax.ShapeDtypeStruct((slots, rows + 12 * quads, panels), jnp.bfloat16),
            jax.ShapeDtypeStruct((row_count,), i32),
            jax.ShapeDtypeStruct((row_count,), i32),
            jax.ShapeDtypeStruct((slots,), i32),
            jax.ShapeDtypeStruct((slots,), i32),
            jax.ShapeDtypeStruct((2,), i32),
        ),
        in_specs=[SM, SM, VM, VM],
        out_specs=(VM, SM, SM, SM, SM, SM),
        scratch_shapes=[
            pltpu.SMEM((peers,), i32),
            pltpu.SMEM((slots,), i32),
            pltpu.SMEM((slots,), i32),
        ],
        compiler_params=PARAMS,
    )(me, pairs.T.reshape(-1), own_geom, density)
    far = lax.all_to_all(send, "clus", split_axis=0, concat_axis=0, tiled=True)
    own_blocks = (panel_count + (LANES - 1)) // LANES
    info = jnp.concatenate([quad.astype(i32).reshape(1), panel_count])
    near = run_pairs(
        0, quads, (counts, ltgt, lsrc, own_blocks), (tpts, own_geom, density), 16 << 30
    )
    return run_pairs(1, quads, (counts, rtgt, rsrc, info), (tpts, far, near), 6 << 30)


def solution(mesh):
    return jax.shard_map(
        shards,
        mesh=mesh,
        in_specs=(
            P(("case", "clus"), None, None),
            P(("case", "clus"), "quad", None, None),
            P(("case", "clus"), "quad", None),
            P(("case", "clus"), None, None),
            P(("case", "clus"), None),
            P(("case", "clus")),
        ),
        out_specs=P(("case", "clus"), None, "quad"),
        check_vma=False,
    )
```

```python
import functools
import math

import jax
import jax.numpy as jnp
import numpy as np
from jax import lax
from jax.experimental import pallas as pl
from jax.experimental.pallas import tpu as pltpu
from jax.sharding import PartitionSpec as P

SLOTS = 2
MACH = 0.3
BETA_SQ = 1.0 - MACH * MACH
TURNS = 8000.0 / 340.0 / BETA_SQ
SOFT = (0.003 * TURNS) ** 2
AMP = TURNS / (4.0 * math.pi)
MAGIC = 12582912.0
LANES = 128
CHUNK = 16
DEPTH = 32
MIDDLE = 0.15


def fit_half_turn(count):
    z = 0.125 - 0.125 * np.cos(np.pi * (np.arange(200) + 0.5) / 200)
    f = np.sqrt(z)
    cheb = np.polynomial.chebyshev.Chebyshev
    poly = np.polynomial.Polynomial
    out = []
    for y in (np.sqrt(2) * np.sin(np.pi * f) / f, np.sqrt(2) * np.cos(np.pi * f)):
        fitted = cheb.fit(z, y, count - 1, domain=[0, 0.25])
        out.append([float(v) for v in fitted.convert(kind=poly).coef])
    return out


SIN_C, COS_C = fit_half_turn(4)


def three_parts(value):
    hi = value.astype(jnp.bfloat16).astype(jnp.float32)
    mid = (value - hi).astype(jnp.bfloat16).astype(jnp.float32)
    return hi, mid, value - hi - mid


def horner(coefs, z):
    value = coefs[-1]
    for c in coefs[-2::-1]:
        value = value * z + c
    return value


def plan_kernel(
    clusters, peers, me_ref, pairs_ref, geom_ref, dens_ref,
    send_ref, ltgt, lsrc, rtgt, rsrc, counts, cnt, key, tgt,
):
    rows = pairs_ref.shape[0] // 2
    drows = dens_ref.shape[1]
    me = me_ref[0]
    first = me * clusters
    total = peers * clusters

    def clear(p, carry):
        cnt[p] = 0
        return carry

    lax.fori_loop(0, peers, clear, 0)

    def more(state):
        return (state[0] < rows) & (pairs_ref[jnp.minimum(state[0], rows - 1)] >= 0)

    def one_row(state):
        r, n_local = state
        a = pairs_ref[r]
        b = pairs_ref[rows + r]
        owner = lax.div(b, jnp.int32(clusters))
        local = owner == me

        @pl.when(local)
        def _():
            ltgt[n_local] = a - first
            lsrc[n_local] = b - first

        @pl.when(owner != me)
        def _():
            mine = jnp.minimum(a, b) * total + jnp.maximum(a, b)
            have = cnt[owner]
            base = owner * SLOTS
            front = (have > 0) & (mine < key[base])

            @pl.when(front)
            def _():
                key[base + 1] = key[base]
                tgt[base + 1] = tgt[base]

            at = jnp.where(front | (have == 0), base, base + 1)
            key[at] = mine
            tgt[at] = a - first
            cnt[owner] = have + 1

        return r + 1, n_local + local.astype(jnp.int32)

    counts[0] = lax.while_loop(more, one_row, (jnp.int32(0), jnp.int32(0)))[1]

    def one_slot(i, n_remote):
        p = lax.div(i, jnp.int32(SLOTS))
        filled = (i - p * SLOTS) < cnt[p]

        @pl.when(filled)
        def _():
            c = tgt[i]
            send_ref[i, pl.ds(0, drows), :] = dens_ref[c]
            rest = jnp.concatenate([geom_ref[q, c] for q in range(geom_ref.shape[0])], axis=0)
            for part in range(3):
                piece = rest.astype(jnp.bfloat16)
                send_ref[i, pl.ds(drows + part * rest.shape[0], rest.shape[0]), :] = piece
                rest = rest - piece.astype(jnp.float32)
            rtgt[n_remote] = c
            rsrc[n_remote] = i

        return n_remote + filled.astype(jnp.int32)

    counts[1] = lax.fori_loop(0, peers * SLOTS, one_slot, jnp.int32(0))


def pair_kernel(which, points, counts, tgt, src, *rest):
    if which == 0:
        nblk, tpts_ref, geom_ref, dens_ref, acc_ref, tb, amat, bmat, sq_ref, tile_a, tile_b = rest
    else:
        (info, tpts_ref, dens_ref, prev_ref, out_ref, acc_ref, tb, amat, bmat, sq_ref,
         tile_a, tile_b, geom_ref, nblk) = rest
    clusters, width = tpts_ref.shape[0], tpts_ref.shape[1]
    quarter = width // 2
    drows = acc_ref.shape[2]
    tiles = (tile_a, tile_b)

    def source(q, s, comp, cols):
        if which == 0:
            return geom_ref[q, s, pl.ds(comp, 1), cols]
        return geom_ref[s, pl.ds(4 * q + comp, 1), cols]

    def source_factor(s, q, g):
        x, y, z = g[0:1], g[1:2], g[2:3]
        norm = x * x + (y * y + (z * z + SOFT))
        hi, mid, lo = three_parts(jnp.concatenate([-2.0 * x, -2.0 * y, -2.0 * z, norm], axis=0))
        ones = jnp.ones_like(hi)
        rows = jnp.concatenate([hi, mid, hi, mid, lo, hi, ones, ones], axis=0)
        bmat[s * points + q] = rows.astype(jnp.bfloat16)

    def unpack(i, carry):
        s = src[i]
        n = 4 * points
        p0, p1, p2 = [dens_ref[s, pl.ds(drows + k * n, n), :].astype(jnp.float32) for k in range(3)]
        whole = p0 + (p1 + p2)
        geom_ref[s] = whole
        block_no = lax.broadcasted_iota(jnp.int32, whole.shape, 1) // LANES + 1
        weight_row = lax.rem(lax.broadcasted_iota(jnp.int32, whole.shape, 0), 4) == 3
        reach = jnp.where(weight_row & (whole != 0), block_no.astype(jnp.float32), 0.0)
        nblk[s] = jnp.max(reach).astype(jnp.int32)
        for q in range(points):
            source_factor(s, q, whole[4 * q : 4 * q + 4])
        return carry

    if which == 1:
        lax.fori_loop(0, counts[1], unpack, 0)

    def fill(c, carry):
        pts = tpts_ref[c]
        x, y, z = pts[:, 0:1], pts[:, 1:2], pts[:, 2:3]
        tb[c] = jnp.broadcast_to(MACH * x, (width, LANES))
        column = lax.broadcasted_iota(jnp.int32, (width, DEPTH), 1)
        comp, group = lax.rem(column, 4), lax.div(column, jnp.int32(4))
        value = jnp.where(comp == 0, x, jnp.where(comp == 1, y, jnp.where(comp == 2, z, 1.0)))
        hi, mid, lo = three_parts(value)
        thi, tmid, tlo = three_parts(
            jnp.broadcast_to(x * x + (y * y + z * z), (width, DEPTH))
        )
        norm = jnp.where(
            comp == 0, thi, jnp.where(comp == 1, tmid, jnp.where(comp == 2, tlo, 0.0))
        )
        first = (group == 0) | (group == 1) | (group == 4)
        second = (group == 2) | (group == 3)
        factor = jnp.where(first, hi, jnp.where(second, mid, jnp.where(group == 5, lo, 0.0)))
        amat[c] = jnp.where(group == 6, norm, factor).astype(jnp.bfloat16)
        if which == 0:
            for q in range(points):
                source_factor(c, q, geom_ref[q, c])
        if which == 0:
            acc_ref[c] = jnp.zeros(acc_ref.shape[1:], jnp.float32)
        else:
            acc_ref[c] = prev_ref[c]
        return carry

    lax.fori_loop(0, clusters, fill, 0)

    def squares(t, s, sb, part):
        cols = pl.ds(pl.multiple_of(sb * LANES, LANES), LANES)
        for q in range(points):
            sq_ref[q, part, :] = jnp.dot(
                amat[t, part, :], bmat[s * points + q, :, cols],
                preferred_element_type=jnp.float32,
            )

    @pl.when(counts[which] > 0)
    def _():
        squares(tgt[0], src[0], 0, pl.ds(0, width))

    def one_pair(i, carry):
        t = tgt[i]
        s = src[i]
        blocks = jnp.maximum(nblk[s], 1)
        after = jnp.minimum(i + 1, counts[which] - 1)

        def one_block(sb, inner):
            cols = pl.ds(pl.multiple_of(sb * LANES, LANES), LANES)
            last = sb + 1 >= blocks
            t_next = jnp.where(last, tgt[after], t)
            s_next = jnp.where(last, src[after], s)
            sb_next = jnp.where(last, 0, sb + 1)
            shift = [MACH * source(q, s, 0, cols) for q in range(points)]
            for ch in range(width // CHUNK):
                rows = pl.ds(ch * CHUNK, CHUNK)
                mtx = tb[t, rows, :]
                re = im = None
                for q in range(points):
                    w = source(q, s, 3, cols)
                    sq = sq_ref[q, rows, :]
                    inv = lax.rsqrt(sq)
                    turns = sq * inv + (shift[q] - mtx)
                    f = turns - ((turns + MAGIC) - MAGIC)
                    z = f * f
                    sn = f * horner(SIN_C, z)
                    cs = horner(COS_C, z)
                    amp = w * inv
                    asn = amp * sn
                    kr = amp - asn * sn
                    ki = asn * cs
                    re = kr if re is None else re + kr
                    im = ki if im is None else im + ki
                tile = tiles[ch * CHUNK // quarter]
                at = ch * CHUNK % quarter
                tile[pl.ds(at, CHUNK), :] = re.astype(jnp.bfloat16)
                tile[pl.ds(quarter + at, CHUNK), :] = im.astype(jnp.bfloat16)
                if at + CHUNK == quarter:
                    part = pl.ds(ch * CHUNK // quarter * width, width)
                    acc_ref[t, part, :] += lax.dot_general(
                        tile[...], dens_ref[s, pl.ds(0, drows), cols], (((1,), (1,)), ((), ())),
                        preferred_element_type=jnp.float32,
                    )
                    squares(t_next, s_next, sb_next, pl.ds(ch * CHUNK // quarter * quarter, quarter))
            return inner

        lax.fori_loop(0, blocks, one_block, 0)
        return carry

    lax.fori_loop(0, counts[which], one_pair, 0)

    if which == 1:
        half = out_ref.shape[1] // 2
        lane = lax.broadcasted_iota(jnp.int32, (half, width), 1) + info[0] * width

        def finish(c, carry):
            live = lane < info[c + 1]
            p, q = [
                jnp.concatenate(
                    [acc_ref[c, pl.ds(g * width + o, quarter), :] for g in range(2)], axis=0
                ).T
                for o in (0, quarter)
            ]
            out_ref[c, pl.ds(0, half), :] = jnp.where(live, p[:half] - q[half:], 0.0)
            out_ref[c, pl.ds(half, half), :] = jnp.where(live, p[half:] + q[:half], 0.0)
            return carry

        lax.fori_loop(0, clusters, finish, 0)


VM = pl.BlockSpec(memory_space=pltpu.VMEM)
SM = pl.BlockSpec(memory_space=pltpu.SMEM)
PARAMS = pltpu.CompilerParams(vmem_limit_bytes=40 << 20)


def run_pairs(which, points, lists, arrays, est):
    tpts, dens = arrays[0], arrays[-1] if which == 0 else arrays[1]
    clusters, width = tpts.shape[0], tpts.shape[1]
    panels = dens.shape[2]
    rows = dens.shape[1] - (12 * points if which == 1 else 0)
    acc_shape = (clusters, 2 * width, rows)
    scratch = [
        pltpu.VMEM((clusters, width, LANES), jnp.float32),
        pltpu.VMEM((clusters, width, DEPTH), jnp.bfloat16),
        pltpu.VMEM((dens.shape[0] * points, DEPTH, panels), jnp.bfloat16),
        pltpu.VMEM((points, width, LANES), jnp.float32),
        pltpu.VMEM((width, LANES), jnp.bfloat16),
        pltpu.VMEM((width, LANES), jnp.bfloat16),
    ]
    out_shape = acc_shape
    if which == 1:
        out_shape = (clusters, rows, width)
        scratch = [pltpu.VMEM(acc_shape, jnp.float32)] + scratch + [
            pltpu.VMEM((dens.shape[0], 4 * points, panels), jnp.float32),
            pltpu.SMEM((dens.shape[0],), jnp.int32),
        ]
    return pl.pallas_call(
        functools.partial(pair_kernel, which, points),
        out_shape=jax.ShapeDtypeStruct(out_shape, jnp.float32),
        in_specs=[SM] * len(lists) + [VM] * len(arrays),
        out_specs=VM,
        scratch_shapes=scratch,
        compiler_params=PARAMS,
        cost_estimate=pl.CostEstimate(flops=est, bytes_accessed=4 << 20, transcendentals=0),
    )(*lists, *arrays)


def shards(targets, source_xyz, source_wts, density, pairs, panel_count):
    clusters, _, panels = targets.shape
    peers = lax.axis_size("clus")
    quads = lax.axis_size("quad")
    width = panels // quads
    rows = density.shape[1]
    quad = lax.axis_index("quad")
    i32 = jnp.int32
    comp = lax.broadcasted_iota(i32, (1, 3, 1), 1)
    scale = jnp.where(comp == 0, jnp.float32(TURNS), jnp.float32(TURNS * math.sqrt(BETA_SQ)))
    live = jnp.arange(panels, dtype=i32)[None, :] < panel_count[:, None]
    packed = jnp.concatenate(
        [
            (source_xyz[:, 0] - MIDDLE) * scale,
            jnp.where(live, source_wts[:, 0] * AMP, 0.0)[:, None, :],
        ],
        axis=1,
    )
    own_geom = lax.all_gather(packed, "quad", axis=0)
    mine = lax.dynamic_slice_in_dim(targets, quad * width, width, 2)
    tpts = jnp.transpose((mine - MIDDLE) * scale, (0, 2, 1))
    me = lax.axis_index("clus").astype(i32).reshape(1)
    slots = peers * SLOTS
    row_count = pairs.shape[0]
    send, ltgt, lsrc, rtgt, rsrc, counts = pl.pallas_call(
        functools.partial(plan_kernel, clusters, peers),
        out_shape=(
            jax.ShapeDtypeStruct((slots, rows + 12 * quads, panels), jnp.bfloat16),
            jax.ShapeDtypeStruct((row_count,), i32),
            jax.ShapeDtypeStruct((row_count,), i32),
            jax.ShapeDtypeStruct((slots,), i32),
            jax.ShapeDtypeStruct((slots,), i32),
            jax.ShapeDtypeStruct((2,), i32),
        ),
        in_specs=[SM, SM, VM, VM],
        out_specs=(VM, SM, SM, SM, SM, SM),
        scratch_shapes=[
            pltpu.SMEM((peers,), i32),
            pltpu.SMEM((slots,), i32),
            pltpu.SMEM((slots,), i32),
        ],
        compiler_params=PARAMS,
    )(me, pairs.T.reshape(-1), own_geom, density)
    far = lax.all_to_all(send, "clus", split_axis=0, concat_axis=0, tiled=True)
    own_blocks = (panel_count + (LANES - 1)) // LANES
    info = jnp.concatenate([quad.astype(i32).reshape(1), panel_count])
    near = run_pairs(
        0, quads, (counts, ltgt, lsrc, own_blocks), (tpts, own_geom, density), 16 << 30
    )
    return run_pairs(1, quads, (counts, rtgt, rsrc, info), (tpts, far, near), 6 << 30)


def solution(mesh):
    return jax.shard_map(
        shards,
        mesh=mesh,
        in_specs=(
            P(("case", "clus"), None, None),
            P(("case", "clus"), "quad", None, None),
            P(("case", "clus"), "quad", None),
            P(("case", "clus"), None, None),
            P(("case", "clus"), None),
            P(("case", "clus")),
        ),
        out_specs=P(("case", "clus"), None, "quad"),
        check_vma=False,
    )
```

```python
import functools
import math

import jax
import jax.numpy as jnp
import numpy as np
from jax import lax
from jax.experimental import pallas as pl
from jax.experimental.pallas import tpu as pltpu
from jax.sharding import PartitionSpec as P

SLOTS = 2
MACH = 0.3
BETA_SQ = 1.0 - MACH * MACH
TURNS = 8000.0 / 340.0 / BETA_SQ
SOFT = (0.003 * TURNS) ** 2
AMP = TURNS / (4.0 * math.pi)
MAGIC = 12582912.0
LANES = 128
CHUNK = 16
DEPTH = 32
MIDDLE = 0.15


def fit_half_turn(count):
    z = 0.125 - 0.125 * np.cos(np.pi * (np.arange(200) + 0.5) / 200)
    f = np.sqrt(z)
    cheb = np.polynomial.chebyshev.Chebyshev
    poly = np.polynomial.Polynomial
    out = []
    for y in (np.sqrt(2) * np.sin(np.pi * f) / f, np.sqrt(2) * np.cos(np.pi * f)):
        fitted = cheb.fit(z, y, count - 1, domain=[0, 0.25])
        out.append([float(v) for v in fitted.convert(kind=poly).coef])
    return out


SIN_C, COS_C = fit_half_turn(4)


def three_parts(value):
    hi = value.astype(jnp.bfloat16).astype(jnp.float32)
    mid = (value - hi).astype(jnp.bfloat16).astype(jnp.float32)
    return hi, mid, value - hi - mid


def horner(coefs, z):
    value = coefs[-1]
    for c in coefs[-2::-1]:
        value = value * z + c
    return value


def plan_kernel(
    clusters, peers, me_ref, pairs_ref, geom_ref, dens_ref,
    send_ref, ltgt, lsrc, rtgt, rsrc, counts, cnt, key, tgt,
):
    rows = pairs_ref.shape[0] // 2
    drows = dens_ref.shape[1]
    me = me_ref[0]
    first = me * clusters
    total = peers * clusters

    def clear(p, carry):
        cnt[p] = 0
        return carry

    lax.fori_loop(0, peers, clear, 0)

    def more(state):
        return (state[0] < rows) & (pairs_ref[jnp.minimum(state[0], rows - 1)] >= 0)

    def one_row(state):
        r, n_local = state
        a = pairs_ref[r]
        b = pairs_ref[rows + r]
        owner = lax.div(b, jnp.int32(clusters))
        local = owner == me

        @pl.when(local)
        def _():
            ltgt[n_local] = a - first
            lsrc[n_local] = b - first

        @pl.when(owner != me)
        def _():
            mine = jnp.minimum(a, b) * total + jnp.maximum(a, b)
            have = cnt[owner]
            base = owner * SLOTS
            front = (have > 0) & (mine < key[base])

            @pl.when(front)
            def _():
                key[base + 1] = key[base]
                tgt[base + 1] = tgt[base]

            at = jnp.where(front | (have == 0), base, base + 1)
            key[at] = mine
            tgt[at] = a - first
            cnt[owner] = have + 1

        return r + 1, n_local + local.astype(jnp.int32)

    counts[0] = lax.while_loop(more, one_row, (jnp.int32(0), jnp.int32(0)))[1]

    def one_slot(i, n_remote):
        p = lax.div(i, jnp.int32(SLOTS))
        filled = (i - p * SLOTS) < cnt[p]

        @pl.when(filled)
        def _():
            c = tgt[i]
            send_ref[i, pl.ds(0, drows), :] = dens_ref[c]
            rest = jnp.concatenate([geom_ref[q, c] for q in range(geom_ref.shape[0])], axis=0)
            for part in range(3):
                piece = rest.astype(jnp.bfloat16)
                send_ref[i, pl.ds(drows + part * rest.shape[0], rest.shape[0]), :] = piece
                rest = rest - piece.astype(jnp.float32)
            rtgt[n_remote] = c
            rsrc[n_remote] = i

        return n_remote + filled.astype(jnp.int32)

    counts[1] = lax.fori_loop(0, peers * SLOTS, one_slot, jnp.int32(0))


def pair_kernel(which, points, counts, tgt, src, *rest):
    if which == 0:
        nblk, tpts_ref, geom_ref, dens_ref, acc_ref, tb, amat, bmat, sq_ref, tile_a, tile_b = rest
    else:
        (info, tpts_ref, dens_ref, prev_ref, tb, amat, out_ref, acc_ref, bmat, sq_ref,
         tile_a, tile_b, geom_ref, nblk) = rest
    clusters, width = tpts_ref.shape[0], tpts_ref.shape[1]
    quarter = width // 2
    drows = acc_ref.shape[2]
    tiles = (tile_a, tile_b)

    def source(q, s, comp, cols):
        if which == 0:
            return geom_ref[q, s, pl.ds(comp, 1), cols]
        return geom_ref[s, pl.ds(4 * q + comp, 1), cols]

    def source_factor(s, q, g):
        x, y, z = g[0:1], g[1:2], g[2:3]
        norm = x * x + (y * y + (z * z + SOFT))
        hi, mid, lo = three_parts(jnp.concatenate([-2.0 * x, -2.0 * y, -2.0 * z, norm], axis=0))
        ones = jnp.ones_like(hi)
        rows = jnp.concatenate([hi, mid, hi, mid, lo, hi, ones, ones], axis=0)
        bmat[s * points + q] = rows.astype(jnp.bfloat16)

    def unpack(i, carry):
        s = src[i]
        n = 4 * points
        p0, p1, p2 = [dens_ref[s, pl.ds(drows + k * n, n), :].astype(jnp.float32) for k in range(3)]
        whole = p0 + (p1 + p2)
        geom_ref[s] = whole
        block_no = lax.broadcasted_iota(jnp.int32, whole.shape, 1) // LANES + 1
        weight_row = lax.rem(lax.broadcasted_iota(jnp.int32, whole.shape, 0), 4) == 3
        reach = jnp.where(weight_row & (whole != 0), block_no.astype(jnp.float32), 0.0)
        nblk[s] = jnp.max(reach).astype(jnp.int32)
        for q in range(points):
            source_factor(s, q, whole[4 * q : 4 * q + 4])
        return carry

    if which == 1:
        lax.fori_loop(0, counts[1], unpack, 0)

    def fill(c, carry):
        if which == 1:
            acc_ref[c] = prev_ref[c]
            return carry
        acc_ref[c] = jnp.zeros(acc_ref.shape[1:], jnp.float32)
        pts = tpts_ref[c]
        x, y, z = pts[:, 0:1], pts[:, 1:2], pts[:, 2:3]
        tb[c] = jnp.broadcast_to(MACH * x, (width, LANES))
        column = lax.broadcasted_iota(jnp.int32, (width, DEPTH), 1)
        comp, group = lax.rem(column, 4), lax.div(column, jnp.int32(4))
        value = jnp.where(comp == 0, x, jnp.where(comp == 1, y, jnp.where(comp == 2, z, 1.0)))
        hi, mid, lo = three_parts(value)
        thi, tmid, tlo = three_parts(
            jnp.broadcast_to(x * x + (y * y + z * z), (width, DEPTH))
        )
        norm = jnp.where(
            comp == 0, thi, jnp.where(comp == 1, tmid, jnp.where(comp == 2, tlo, 0.0))
        )
        first = (group == 0) | (group == 1) | (group == 4)
        second = (group == 2) | (group == 3)
        factor = jnp.where(first, hi, jnp.where(second, mid, jnp.where(group == 5, lo, 0.0)))
        amat[c] = jnp.where(group == 6, norm, factor).astype(jnp.bfloat16)
        for q in range(points):
            source_factor(c, q, geom_ref[q, c])
        return carry

    lax.fori_loop(0, clusters, fill, 0)

    def squares(t, s, sb, part):
        cols = pl.ds(pl.multiple_of(sb * LANES, LANES), LANES)
        for q in range(points):
            sq_ref[q, part, :] = jnp.dot(
                amat[t, part, :], bmat[s * points + q, :, cols],
                preferred_element_type=jnp.float32,
            )

    @pl.when(counts[which] > 0)
    def _():
        squares(tgt[0], src[0], 0, pl.ds(0, width))

    def one_pair(i, carry):
        t = tgt[i]
        s = src[i]
        blocks = jnp.maximum(nblk[s], 1)
        after = jnp.minimum(i + 1, counts[which] - 1)

        def one_block(sb, inner):
            cols = pl.ds(pl.multiple_of(sb * LANES, LANES), LANES)
            last = sb + 1 >= blocks
            t_next = jnp.where(last, tgt[after], t)
            s_next = jnp.where(last, src[after], s)
            sb_next = jnp.where(last, 0, sb + 1)
            shift = [MACH * source(q, s, 0, cols) for q in range(points)]
            for ch in range(width // CHUNK):
                rows = pl.ds(ch * CHUNK, CHUNK)
                mtx = tb[t, rows, :]
                re = im = None
                for q in range(points):
                    w = source(q, s, 3, cols)
                    sq = sq_ref[q, rows, :]
                    inv = lax.rsqrt(sq)
                    turns = sq * inv + (shift[q] - mtx)
                    f = turns - ((turns + MAGIC) - MAGIC)
                    z = f * f
                    sn = f * horner(SIN_C, z)
                    cs = horner(COS_C, z)
                    amp = w * inv
                    asn = amp * sn
                    kr = amp - asn * sn
                    ki = asn * cs
                    re = kr if re is None else re + kr
                    im = ki if im is None else im + ki
                tile = tiles[ch * CHUNK // quarter]
                at = ch * CHUNK % quarter
                tile[pl.ds(at, CHUNK), :] = re.astype(jnp.bfloat16)
                tile[pl.ds(quarter + at, CHUNK), :] = im.astype(jnp.bfloat16)
                if at + CHUNK == quarter:
                    part = pl.ds(ch * CHUNK // quarter * width, width)
                    acc_ref[t, part, :] += lax.dot_general(
                        tile[...], dens_ref[s, pl.ds(0, drows), cols], (((1,), (1,)), ((), ())),
                        preferred_element_type=jnp.float32,
                    )
                    squares(t_next, s_next, sb_next, pl.ds(ch * CHUNK // quarter * quarter, quarter))
            return inner

        lax.fori_loop(0, blocks, one_block, 0)
        return carry

    lax.fori_loop(0, counts[which], one_pair, 0)

    if which == 1:
        half = out_ref.shape[1] // 2
        lane = lax.broadcasted_iota(jnp.int32, (half, width), 1) + info[0] * width

        def finish(c, carry):
            live = lane < info[c + 1]
            p, q = [
                jnp.concatenate(
                    [acc_ref[c, pl.ds(g * width + o, quarter), :] for g in range(2)], axis=0
                ).T
                for o in (0, quarter)
            ]
            out_ref[c, pl.ds(0, half), :] = jnp.where(live, p[:half] - q[half:], 0.0)
            out_ref[c, pl.ds(half, half), :] = jnp.where(live, p[half:] + q[:half], 0.0)
            return carry

        lax.fori_loop(0, clusters, finish, 0)


VM = pl.BlockSpec(memory_space=pltpu.VMEM)
SM = pl.BlockSpec(memory_space=pltpu.SMEM)
PARAMS = pltpu.CompilerParams(vmem_limit_bytes=40 << 20)


def run_pairs(which, points, lists, arrays, est):
    tpts, dens = arrays[0], arrays[-1] if which == 0 else arrays[1]
    clusters, width = tpts.shape[0], tpts.shape[1]
    panels = dens.shape[2]
    rows = dens.shape[1] - (12 * points if which == 1 else 0)
    acc_shape = (clusters, 2 * width, rows)
    scratch = [
        pltpu.VMEM((dens.shape[0] * points, DEPTH, panels), jnp.bfloat16),
        pltpu.VMEM((points, width, LANES), jnp.float32),
        pltpu.VMEM((width, LANES), jnp.bfloat16),
        pltpu.VMEM((width, LANES), jnp.bfloat16),
    ]
    out_shape = (
        jax.ShapeDtypeStruct(acc_shape, jnp.float32),
        jax.ShapeDtypeStruct((clusters, width, LANES), jnp.float32),
        jax.ShapeDtypeStruct((clusters, width, DEPTH), jnp.bfloat16),
    )
    if which == 1:
        out_shape = jax.ShapeDtypeStruct((clusters, rows, width), jnp.float32)
        scratch = [pltpu.VMEM(acc_shape, jnp.float32)] + scratch + [
            pltpu.VMEM((dens.shape[0], 4 * points, panels), jnp.float32),
            pltpu.SMEM((dens.shape[0],), jnp.int32),
        ]
    return pl.pallas_call(
        functools.partial(pair_kernel, which, points),
        out_shape=out_shape,
        in_specs=[SM] * len(lists) + [VM] * len(arrays),
        out_specs=VM if which else (VM,) * 3,
        scratch_shapes=scratch,
        compiler_params=PARAMS,
        cost_estimate=pl.CostEstimate(flops=est, bytes_accessed=4 << 20, transcendentals=0),
    )(*lists, *arrays)


def shards(targets, source_xyz, source_wts, density, pairs, panel_count):
    clusters, _, panels = targets.shape
    peers = lax.axis_size("clus")
    quads = lax.axis_size("quad")
    width = panels // quads
    rows = density.shape[1]
    quad = lax.axis_index("quad")
    i32 = jnp.int32
    comp = lax.broadcasted_iota(i32, (1, 3, 1), 1)
    scale = jnp.where(comp == 0, jnp.float32(TURNS), jnp.float32(TURNS * math.sqrt(BETA_SQ)))
    live = jnp.arange(panels, dtype=i32)[None, :] < panel_count[:, None]
    packed = jnp.concatenate(
        [
            (source_xyz[:, 0] - MIDDLE) * scale,
            jnp.where(live, source_wts[:, 0] * AMP, 0.0)[:, None, :],
        ],
        axis=1,
    )
    own_geom = lax.all_gather(packed, "quad", axis=0)
    mine = lax.dynamic_slice_in_dim(targets, quad * width, width, 2)
    tpts = jnp.transpose((mine - MIDDLE) * scale, (0, 2, 1))
    me = lax.axis_index("clus").astype(i32).reshape(1)
    slots = peers * SLOTS
    row_count = pairs.shape[0]
    send, ltgt, lsrc, rtgt, rsrc, counts = pl.pallas_call(
        functools.partial(plan_kernel, clusters, peers),
        out_shape=(
            jax.ShapeDtypeStruct((slots, rows + 12 * quads, panels), jnp.bfloat16),
            jax.ShapeDtypeStruct((row_count,), i32),
            jax.ShapeDtypeStruct((row_count,), i32),
            jax.ShapeDtypeStruct((slots,), i32),
            jax.ShapeDtypeStruct((slots,), i32),
            jax.ShapeDtypeStruct((2,), i32),
        ),
        in_specs=[SM, SM, VM, VM],
        out_specs=(VM, SM, SM, SM, SM, SM),
        scratch_shapes=[
            pltpu.SMEM((peers,), i32),
            pltpu.SMEM((slots,), i32),
            pltpu.SMEM((slots,), i32),
        ],
        compiler_params=PARAMS,
    )(me, pairs.T.reshape(-1), own_geom, density)
    far = lax.all_to_all(send, "clus", split_axis=0, concat_axis=0, tiled=True)
    own_blocks = (panel_count + (LANES - 1)) // LANES
    info = jnp.concatenate([quad.astype(i32).reshape(1), panel_count])
    near = run_pairs(
        0, quads, (counts, ltgt, lsrc, own_blocks), (tpts, own_geom, density), 16 << 30
    )
    return run_pairs(1, quads, (counts, rtgt, rsrc, info), (tpts, far, *near), 6 << 30)


def solution(mesh):
    return jax.shard_map(
        shards,
        mesh=mesh,
        in_specs=(
            P(("case", "clus"), None, None),
            P(("case", "clus"), "quad", None, None),
            P(("case", "clus"), "quad", None),
            P(("case", "clus"), None, None),
            P(("case", "clus"), None),
            P(("case", "clus")),
        ),
        out_specs=P(("case", "clus"), None, "quad"),
        check_vma=False,
    )
```
